32 devices in a mesh: seq: 16 (over z, y, x), head: 2 (over core).
Axes of the slice: x: 2, y: 2, z: 4, core: 2. Of those that a mesh axis runs over, the one named last changes fastest.
Arguments:
- layer_input: bfloat16 [8192, 5376], P('seq', 'head'), may hold values from -6 to 6
- omega_in: bfloat16 [5376, 128], P('head'), may hold values from -0.0078125 to 0.0078125
- upstream: bfloat16 [8192, 5376], P('seq', 'head'), may hold values from -6 to 6
- omega_out: bfloat16 [5376, 128], P('head'), may hold values from -0.0078125 to 0.0078125
- q_raw: bfloat16 [8192, 4096], P('seq', 'head'), may hold values from -6 to 6
- k_raw: bfloat16 [8192, 2048], P('seq', 'head'), may hold values from -6 to 6
- values: bfloat16 [8192, 2048], P('seq', 'head'), may hold values from -6 to 6
- d_out: bfloat16 [8192, 4096], P('seq', 'head'), may hold values from -16 to 16
- q_gain: float32 [128], replicated, may hold values from 0.1 to 1.9
- k_gain: float32 [128], replicated, may hold values from 0.1 to 1.9
Outputs:
- query_grad: bfloat16 [8192, 4096], P('seq', 'head')
- key_grad: bfloat16 [8192, 2048], P('seq', 'head')
- value_grad: bfloat16 [8192, 2048], P('seq', 'head')
- sketch_q: float32 [128, 4096], P('seq', 'head')
- sketch_k: float32 [128, 2048], P('seq', 'head')
- sketch_v: float32 [128, 2048], P('seq', 'head')
- sketch_o: float32 [128, 4096], P('seq', 'head')
The draws below stay inside these ranges and needn't reach their ends.
All inputs are finite; a program needn't handle non-finite values.
Results may differ from the reference program's by a relative error of at most 0.013.
Values may be sent and summed in bfloat16 or wider, within the bound.
A program may use at most 128 MiB of HBM per device.

```python
import jax
import jax.numpy as jnp
from jax import lax

D = 5376
QH = 32
KH = 16
HD = 128
WINDOW = 1024
RANK = 128
TOK_DEV = 512
TOKENS = 8192
HALO_DEV = 2


def steps_of(rng, dims, pieces, smallest, high):
    level = 1.0
    for axis_at, parts in pieces:
        draws = jax.random.uniform(jax.random.fold_in(jax.random.fold_in(rng, 6), axis_at), (parts,), jnp.float32, smallest / len(pieces), high / len(pieces))
        level = level * jnp.repeat(jnp.exp(draws), dims[axis_at] // parts).reshape((-1,) + (1,) * (len(dims) - 1 - axis_at))
    return level


def gaussian(own_key, extent, spread, most, pieces=(), kind=jnp.bfloat16):
    drawn = jax.random.normal(own_key, extent, jnp.float32) * spread
    if len(pieces) > 0:
        drawn = steps_of(own_key, extent, pieces, -0.22, 0.18) * drawn
    return jnp.clip(drawn, min=-most, max=most).astype(kind)


def setup_inputs(seed: int = 0) -> dict:
    key_of = jax.random.split(jax.random.key(seed), 11)
    return {
        "layer_input": gaussian(key_of[0], (TOKENS, D), 1.0, 6.0, ((0, 16), (1, 2))),
        "omega_in": gaussian(key_of[1], (D, RANK), (D * TOKENS // 64) ** -0.5, 0.0078125, ((0, 2),)),
        "upstream": gaussian(key_of[2], (TOKENS, D), 1.0, 6.0, ((0, 16), (1, 2))),
        "omega_out": gaussian(key_of[3], (D, RANK), (D * TOKENS // 64) ** -0.5, 0.0078125, ((0, 2),)),
        "q_raw": gaussian(key_of[4], (TOKENS, QH * HD), 1.0, 6.0, ((0, 16), (1, 2))),
        "k_raw": gaussian(key_of[5], (TOKENS, KH * HD), 1.0, 6.0, ((0, 16), (1, 2))),
        "values": gaussian(key_of[6], (TOKENS, KH * HD), 1.0, 6.0, ((0, 16), (1, 2))),
        "d_out": gaussian(key_of[7], (TOKENS, QH * HD), 4.0, 16.0, ((0, 16), (1, 2))),
        "q_gain": jnp.clip(1.0 + 0.18 * jax.random.normal(key_of[8], (HD,), jnp.float32), 0.1, 1.9),
        "k_gain": jnp.clip(1.0 + 0.18 * jax.random.normal(key_of[9], (HD,), jnp.float32), 0.1, 1.9),
    }


score_scale = 168.0 ** (-0.5)
epsilon = 1e-06
rope_base = 10000.0

def prepare(raw_input, gain, positions):
    mean_square = lax.optimization_barrier(jnp.mean(raw_input * raw_input, axis=-1, keepdims=True))
    normed = raw_input * lax.rsqrt(mean_square + epsilon) * gain
    half_dim = raw_input.shape[-1] // 2
    inverse_freq = rope_base ** (-(jnp.arange(half_dim, dtype=jnp.float32) * 2.0 / raw_input.shape[-1]))
    angles = positions.astype(jnp.float32)[:, None] * inverse_freq[None, :]
    cos_table = jnp.cos(angles)[:, None, :]
    sin_table = jnp.sin(angles)[:, None, :]
    lower_half = normed[..., :half_dim]
    upper_half = normed[..., half_dim:]
    return jnp.concatenate([lower_half * cos_table - upper_half * sin_table, upper_half * cos_table + lower_half * sin_table], axis=-1)

def head_core(query_rows, key_rows, value_rows, grad_rows, allowed):
    scores = score_scale * jnp.dot(query_rows, key_rows.T, preferred_element_type=jnp.float32)
    exp_scores = jnp.where(allowed, jnp.exp(scores), 0.0)
    probs = exp_scores / lax.optimization_barrier(jnp.sum(exp_scores, axis=-1, keepdims=True))
    probs_low = probs.astype(jnp.bfloat16)
    attn_rows = jnp.dot(probs_low, value_rows, preferred_element_type=jnp.float32).astype(jnp.bfloat16)
    grad_probs = jnp.dot(grad_rows, value_rows.T, preferred_element_type=jnp.float32)
    row_delta = lax.optimization_barrier(jnp.sum(probs * grad_probs, axis=-1, keepdims=True))
    grad_low = (probs * (grad_probs - row_delta)).astype(jnp.bfloat16)
    query_grad = score_scale * jnp.dot(grad_low, key_rows, preferred_element_type=jnp.float32)
    key_grad = score_scale * jnp.dot(grad_low.T, query_rows, preferred_element_type=jnp.float32)
    value_grad = jnp.dot(probs_low.T, grad_rows, preferred_element_type=jnp.float32)
    return (attn_rows, query_grad, key_grad, value_grad)

def reference(layer_input, omega_in, upstream, omega_out, q_raw, k_raw, values, d_out, q_gain, k_gain):
    tokens = q_raw.shape[0]
    group_size = QH // KH
    ext_rows = HALO_DEV * TOK_DEV
    span_rows = ext_rows + TOK_DEV
    positions = jnp.arange(tokens, dtype=jnp.int32)
    query_f = q_raw.astype(jnp.float32).reshape(tokens, QH, HD)
    key_f = k_raw.astype(jnp.float32).reshape(tokens, KH, HD)
    query_full, query_back = jax.vjp(lambda raw_input: prepare(raw_input, q_gain, positions), query_f)
    key_full, key_back = jax.vjp(lambda raw_input: prepare(raw_input, k_gain, positions), key_f)
    query_prep = query_full.astype(jnp.bfloat16)
    key_prep = key_full.astype(jnp.bfloat16)
    key_pad = jnp.concatenate([jnp.zeros((ext_rows, KH, HD), jnp.bfloat16), key_prep], axis=0)
    value_pad = jnp.concatenate([jnp.zeros((ext_rows, KH, HD), jnp.bfloat16), values.reshape(tokens, KH, HD)], axis=0)
    grad_all = d_out.reshape(tokens, QH, HD)
    row_index = jnp.arange(TOK_DEV, dtype=jnp.int32)[:, None]
    col_index = jnp.arange(span_rows, dtype=jnp.int32)[None, :]
    gap = row_index - col_index + ext_rows

    def block_step(carried, block_index):
        key_acc, value_acc = carried
        begin_row = block_index * TOK_DEV
        key_pos = begin_row - ext_rows + col_index
        allowed = (key_pos >= 0) & (gap >= 0) & (gap < WINDOW)
        query_blk = lax.dynamic_slice_in_dim(query_prep, begin_row, TOK_DEV, 0).transpose(1, 0, 2)
        grad_blk = lax.dynamic_slice_in_dim(grad_all, begin_row, TOK_DEV, 0).transpose(1, 0, 2)
        key_blk = lax.dynamic_slice_in_dim(key_pad, begin_row, span_rows, 0).transpose(1, 0, 2)
        value_blk = lax.dynamic_slice_in_dim(value_pad, begin_row, span_rows, 0).transpose(1, 0, 2)
        key_rep = jnp.repeat(key_blk, group_size, axis=0)
        value_rep = jnp.repeat(value_blk, group_size, axis=0)
        attn_blk, query_grad, key_grad, value_grad = lax.map(lambda items: head_core(items[0], items[1], items[2], items[3], allowed), (query_blk, key_rep, value_rep, grad_blk))
        key_sum = key_grad.reshape(KH, group_size, span_rows, HD).sum(axis=1).transpose(1, 0, 2)
        value_sum = value_grad.reshape(KH, group_size, span_rows, HD).sum(axis=1).transpose(1, 0, 2)
        key_acc = lax.dynamic_update_slice_in_dim(key_acc, lax.dynamic_slice_in_dim(key_acc, begin_row, span_rows, 0) + key_sum, begin_row, 0)
        value_acc = lax.dynamic_update_slice_in_dim(value_acc, lax.dynamic_slice_in_dim(value_acc, begin_row, span_rows, 0) + value_sum, begin_row, 0)
        return ((key_acc, value_acc), (attn_blk, query_grad))
    zero_acc = jnp.zeros((ext_rows + tokens, KH, HD), jnp.float32)
    (key_acc, value_acc), (attn_all, query_all) = lax.scan(block_step, (zero_acc, zero_acc), jnp.arange(tokens // TOK_DEV, dtype=jnp.int32))
    attn_out = attn_all.transpose(0, 2, 1, 3).reshape(tokens, QH * HD)
    query_grad_prep = query_all.transpose(0, 2, 1, 3).reshape(tokens, QH, HD)
    query_grad = query_back(query_grad_prep)[0].reshape(tokens, QH * HD).astype(jnp.bfloat16)
    key_grad = key_back(key_acc[ext_rows:])[0].reshape(tokens, KH * HD).astype(jnp.bfloat16)
    value_grad = value_acc[ext_rows:].reshape(tokens, KH * HD).astype(jnp.bfloat16)
    x_sketch = jnp.dot(layer_input, omega_in, preferred_element_type=jnp.float32).astype(jnp.bfloat16)
    dy_sketch = jnp.dot(upstream, omega_out, preferred_element_type=jnp.float32).astype(jnp.bfloat16)
    sketch_q = jnp.dot(x_sketch.T, query_grad, preferred_element_type=jnp.float32)
    sketch_k = jnp.dot(x_sketch.T, key_grad, preferred_element_type=jnp.float32)
    sketch_v = jnp.dot(x_sketch.T, value_grad, preferred_element_type=jnp.float32)
    sketch_o = jnp.dot(dy_sketch.T, attn_out, preferred_element_type=jnp.float32)
    return (query_grad, key_grad, value_grad, sketch_q, sketch_k, sketch_v, sketch_o)
```

```python
import functools
import math

import jax
import jax.numpy as jnp
from jax import lax
from jax.experimental import pallas as pl
from jax.experimental.pallas import tpu as pltpu
from jax.sharding import PartitionSpec as P

WINDOW = 1024
SCALE = 168.0 ** (-0.5)
EPSILON = 1e-06
ROPE_BASE = 10000.0
NT = (((1,), (1,)), ((), ()))
CHUNKS = 2


def from_behind(shard, axis, by):
    count = lax.axis_size(axis)
    pairs = [(i, i + by) for i in range(count) if 0 <= i + by < count]
    return lax.ppermute(shard, axis, pairs)


def dot(a, b):
    return jnp.dot(a, b, preferred_element_type=jnp.float32)


def dot_nt(a, b):
    return lax.dot_general(a, b, NT, preferred_element_type=jnp.float32)


def swap_halves(x):
    return pltpu.roll(x, x.shape[-1] // 2, 1)


def norm_parts(raw):
    rstd = lax.rsqrt(jnp.mean(raw * raw, axis=-1, keepdims=True) + EPSILON)
    return raw * rstd, rstd


def rotate(normed, cos, sin):
    return normed * cos + swap_halves(normed) * sin


def prepare_back(grad, unit, rstd, gain, cos, sin):
    inner = (grad * cos + swap_halves(grad * sin)) * gain
    return rstd * (inner - unit * jnp.mean(inner * unit, axis=-1, keepdims=True))


def attention_kernel(
    valid, cos, sin, q_gain, k_gain, x_t, dy_t, q, d_out, near, far, k_own, v_own, *rest
):
    (query_out, own_out, near_out, far_out, sketch_out, k_s, v_s, kt_s, vt_s, dk_s, dv_s,
     e_s, dp_s, p_s, ds_s) = rest[-15:]
    tok = q.shape[0]
    hd = q_gain.shape[1]
    group = q.shape[1] // hd
    sub = tok // 2
    span = 3 * tok
    band = 5 * sub
    cols = group * sub
    exponent = SCALE * math.log2(math.e)

    for part, raw, val in ((0, far[0], far[1]), (1, near[0], near[1]), (2, k_own[...], v_own[...])):
        rows = pl.ds(part * tok, tok)
        unit, _ = norm_parts(raw.astype(jnp.float32))
        prep = rotate(unit * k_gain[...], cos[rows, :], sin[rows, :])
        k_s[rows, :] = prep.astype(jnp.bfloat16)
        kt_s[:, part * tok : (part + 1) * tok] = prep.T.astype(jnp.bfloat16)
        v_s[rows, :] = val
        vt_s[:, part * tok : (part + 1) * tok] = val.astype(jnp.float32).T.astype(jnp.bfloat16)

    key_at = lax.broadcasted_iota(jnp.int32, (sub, cols), 0)
    query_at = lax.broadcasted_iota(jnp.int32, (sub, cols), 1) % sub
    older = key_at > query_at
    weight = jnp.where(older, valid[1], 1.0)

    for i in range(2):
        rows = slice(i * sub, (i + 1) * sub)
        own_rows = pl.ds(2 * tok + i * sub, sub)
        q_cos, q_sin = cos[own_rows, :], sin[own_rows, :]
        units = []
        preps = []
        for h in range(group):
            unit, rstd = norm_parts(q[rows, h * hd : (h + 1) * hd].astype(jnp.float32))
            units.append((unit, rstd))
            preps.append(rotate(unit * q_gain[...], q_cos, q_sin).astype(jnp.bfloat16))
        query = jnp.concatenate(preps, axis=0)
        grad = jnp.concatenate([d_out[rows, h * hd : (h + 1) * hd] for h in range(group)], axis=0)

        total = jnp.zeros((1, cols), jnp.float32)
        mixed = jnp.zeros((1, cols), jnp.float32)
        for t in range(4):
            at = slice((i + t) * sub, (i + t + 1) * sub)
            score = dot_nt(k_s[at, :], query)
            grad_p = dot_nt(v_s[at, :], grad)
            if t == 0:
                last = slice((i + 4) * sub, (i + 5) * sub)
                score = jnp.where(older, score, dot_nt(k_s[last, :], query))
                grad_p = jnp.where(older, grad_p, dot_nt(v_s[last, :], grad))
            e = jnp.exp2(score * exponent)
            here = slice(t * sub, (t + 1) * sub)
            e_s[i, here, :] = e
            dp_s[i, here, :] = grad_p
            mixed = mixed + jnp.sum(e * grad_p, axis=0, keepdims=True)
            if t == 0:
                total = total + jnp.sum(e * weight, axis=0, keepdims=True)
            else:
                part = jnp.sum(e, axis=0, keepdims=True)
                shard = (i + t) // 2
                total = total + (part if shard == 2 else part * valid[1 - shard])
        inverse = 1.0 / total
        delta = mixed * inverse
        for t in range(4):
            here = slice(t * sub, (t + 1) * sub)
            prob = e_s[i, here, :] * inverse
            ds = prob * (dp_s[i, here, :] - delta)
            if t == 0:
                last = slice(4 * sub, 5 * sub)
                p_s[i, here, :] = jnp.where(older, prob, 0.0).astype(jnp.bfloat16)
                p_s[i, last, :] = jnp.where(older, 0.0, prob).astype(jnp.bfloat16)
                ds_s[i, here, :] = jnp.where(older, ds, 0.0).astype(jnp.bfloat16)
                ds_s[i, last, :] = jnp.where(older, 0.0, ds).astype(jnp.bfloat16)
            else:
                p_s[i, here, :] = prob.astype(jnp.bfloat16)
                ds_s[i, here, :] = ds.astype(jnp.bfloat16)

        keys = slice(i * sub, i * sub + band)
        dv = dot(p_s[i], grad)
        dk = dot(ds_s[i], query)
        if i == 0:
            dv_s[:band, :] = dv
            dk_s[:band, :] = dk
            dv_s[band:, :] = jnp.zeros((span - band, hd), jnp.float32)
            dk_s[band:, :] = jnp.zeros((span - band, hd), jnp.float32)
        else:
            dv_s[keys, :] += dv
            dk_s[keys, :] += dk
        attn_t = dot(vt_s[:, keys], p_s[i]).astype(jnp.bfloat16)
        dq = dot(kt_s[:, keys], ds_s[i]).T * SCALE
        for h in range(group):
            unit, rstd = units[h]
            part = prepare_back(
                dq[h * sub : (h + 1) * sub, :], unit, rstd, q_gain[...], q_cos, q_sin
            ).astype(jnp.bfloat16)
            query_out[rows, h * hd : (h + 1) * hd] = part
            sk_q = dot(x_t[:, 2 * tok + i * sub : 2 * tok + (i + 1) * sub], part)
            sk_o = dot_nt(dy_t[:, rows], attn_t[:, h * sub : (h + 1) * sub])
            to_q = slice(h * hd, (h + 1) * hd)
            to_o = slice((group + 2 + h) * hd, (group + 3 + h) * hd)
            if i == 0:
                sketch_out[0, :, to_q] = sk_q
                sketch_out[0, :, to_o] = sk_o
            else:
                sketch_out[0, :, to_q] += sk_q
                sketch_out[0, :, to_o] += sk_o

    sk_k = jnp.zeros((x_t.shape[0], hd), jnp.float32)
    sk_v = jnp.zeros((x_t.shape[0], hd), jnp.float32)
    for part, raw, out in ((0, far[0], far_out), (1, near[0], near_out), (2, k_own[...], own_out)):
        rows = pl.ds(part * tok, tok)
        unit, rstd = norm_parts(raw.astype(jnp.float32))
        dk = prepare_back(
            dk_s[rows, :] * SCALE, unit, rstd, k_gain[...], cos[rows, :], sin[rows, :]
        )
        dv = dv_s[rows, :]
        out[0] = dk.astype(out.dtype)
        out[1] = dv.astype(out.dtype)
        xs = x_t[:, part * tok : (part + 1) * tok]
        sk_k = sk_k + dot(xs, dk.astype(jnp.bfloat16))
        sk_v = sk_v + dot(xs, dv.astype(jnp.bfloat16))
    sketch_out[0, :, group * hd : (group + 1) * hd] = sk_k
    sketch_out[0, :, (group + 1) * hd : (group + 2) * hd] = sk_v


def attention(chunk, heads, valid, cos, sin, q_gain, k_gain, x_t, dy_t, q_raw, d_out, near, far,
              k_raw, values, earlier):
    tok, q_cols = q_raw.shape
    hd = q_gain.shape[1]
    group = q_cols // k_raw.shape[1]
    rank = x_t.shape[0]
    wide = group * hd
    first = chunk * heads
    span, sub = 3 * tok, tok // 2
    whole = lambda *shape: pl.BlockSpec(shape, lambda g: (0,) * len(shape))
    q_spec = pl.BlockSpec((tok, wide), lambda g: (0, first + g))
    k_spec = pl.BlockSpec((tok, hd), lambda g: (0, first + g))
    halo = pl.BlockSpec((2, tok, hd), lambda g: (0, 0, g))
    in_specs = [
        pl.BlockSpec(memory_space=pltpu.SMEM),
        whole(span, hd), whole(span, hd), whole(1, hd), whole(1, hd),
        whole(rank, span), whole(rank, tok),
        q_spec, q_spec, halo, halo, k_spec, k_spec,
    ]
    args = [valid, cos, sin, q_gain, k_gain, x_t, dy_t, q_raw, d_out, near, far, k_raw, values]
    aliases = {}
    if earlier is not None:
        in_specs.append(pl.BlockSpec(memory_space=pl.ANY))
        aliases = {len(args): 0}
        args.append(earlier)
    cols = group * sub
    return pl.pallas_call(
        attention_kernel,
        grid=(heads,),
        in_specs=in_specs,
        out_specs=[q_spec, halo, halo, halo,
                   pl.BlockSpec((1, rank, 2 * wide + 2 * hd), lambda g: (g, 0, 0))],
        out_shape=[
            jax.ShapeDtypeStruct(q_raw.shape, jnp.bfloat16),
            jax.ShapeDtypeStruct((2, tok, heads * hd), jnp.float32),
            jax.ShapeDtypeStruct((2, tok, heads * hd), jnp.bfloat16),
            jax.ShapeDtypeStruct((2, tok, heads * hd), jnp.bfloat16),
            jax.ShapeDtypeStruct((heads, rank, 2 * wide + 2 * hd), jnp.float32),
        ],
        scratch_shapes=[
            pltpu.VMEM((span, hd), jnp.bfloat16),
            pltpu.VMEM((span, hd), jnp.bfloat16),
            pltpu.VMEM((hd, span), jnp.bfloat16),
            pltpu.VMEM((hd, span), jnp.bfloat16),
            pltpu.VMEM((span, hd), jnp.float32),
            pltpu.VMEM((span, hd), jnp.float32),
            pltpu.VMEM((2, 4 * sub, cols), jnp.float32),
            pltpu.VMEM((2, 4 * sub, cols), jnp.float32),
            pltpu.VMEM((2, 5 * sub, cols), jnp.bfloat16),
            pltpu.VMEM((2, 5 * sub, cols), jnp.bfloat16),
        ],
        input_output_aliases=aliases,
        compiler_params=pltpu.CompilerParams(
            dimension_semantics=("arbitrary",), vmem_limit_bytes=48 * 1024 * 1024
        ),
        cost_estimate=pl.CostEstimate(
            flops=heads * 20 * 5 * sub * tok * group * hd,
            bytes_accessed=heads * 4 * tok * hd * 20,
            transcendentals=heads * 4 * sub * tok * group,
        ),
    )(*args)


def scatter_sum(part, order):
    count = lax.axis_size("seq")
    bits = len(order)
    heads, rank, cols = part.shape
    me = lax.axis_index("seq")
    cur = part.reshape((heads,) + (2,) * bits + (rank // count, cols))
    axes = list(range(bits - 1, -1, -1))
    for bit in order:
        axis = 1 + axes.index(bit)
        axes.remove(bit)
        mine = (me >> bit) & 1
        keep = lax.dynamic_index_in_dim(cur, mine, axis, keepdims=False)
        away = lax.dynamic_index_in_dim(cur, 1 - mine, axis, keepdims=False)
        pairs = [(i, i ^ (1 << bit)) for i in range(count)]
        cur = keep + lax.ppermute(away.astype(jnp.bfloat16), "seq", pairs).astype(jnp.float32)
    return cur


def per_device(
    layer_input, omega_in, upstream, omega_out, q_raw, k_raw, values, d_out, q_gain, k_gain
):
    tok = q_raw.shape[0]
    hd = q_gain.shape[0]
    kv_cols = k_raw.shape[1]
    heads_kv = kv_cols // hd
    group = q_raw.shape[1] // kv_cols
    per_chunk = heads_kv // CHUNKS
    c_cols = per_chunk * hd
    me = lax.axis_index("seq")
    count = lax.axis_size("seq")

    halos = []
    for c in range(CHUNKS):
        pair = jnp.stack([k_raw[:, c * c_cols : (c + 1) * c_cols],
                          values[:, c * c_cols : (c + 1) * c_cols]])
        halos.append((from_behind(pair, "seq", 1), from_behind(pair, "seq", 2)))

    partial_x = dot(layer_input, omega_in)
    partial_y = dot(upstream, omega_out)
    summed_x, summed_y = lax.psum((partial_x, partial_y), "head")
    x_sketch = summed_x.astype(jnp.bfloat16)
    dy_t = summed_y.astype(jnp.bfloat16).T
    x_t = x_sketch.T
    x_t = jnp.concatenate([from_behind(x_t, "seq", 2), from_behind(x_t, "seq", 1), x_t], axis=1)

    half = hd // 2
    inverse_freq = ROPE_BASE ** (-(jnp.arange(half, dtype=jnp.float32) * 2.0 / hd))
    positions = (me - 2) * tok + jnp.arange(3 * tok, dtype=jnp.int32)
    angles = positions.astype(jnp.float32)[:, None] * inverse_freq[None, :]
    cos, sin = jnp.cos(angles), jnp.sin(angles)
    cos = jnp.concatenate([cos, cos], axis=1)
    sin = jnp.concatenate([-sin, sin], axis=1)
    valid = jnp.stack([me >= 1, me >= 2]).astype(jnp.float32)

    query_grad = None
    returned = []
    sketches = []
    bits = count.bit_length() - 1
    for c in range(CHUNKS):
        query_grad, own, near, far, sketch = attention(
            c, per_chunk, valid, cos, sin, q_gain[None, :], k_gain[None, :], x_t, dy_t,
            q_raw, d_out, halos[c][0], halos[c][1], k_raw, values, query_grad,
        )
        back = (own, from_behind(near, "seq", -1), from_behind(far, "seq", -2))
        returned.append(back)
        order = list(range(bits))
        if c % 2 == 1 and bits > 1:
            order[0], order[1] = order[1], order[0]
        sketches.append(scatter_sum(sketch, order))

    sums = [(o + n.astype(jnp.float32) + f.astype(jnp.float32)).astype(jnp.bfloat16)
            for o, n, f in returned]
    key_grad = jnp.concatenate([s[0] for s in sums], axis=1)
    value_grad = jnp.concatenate([s[1] for s in sums], axis=1)
    all_sketch = jnp.concatenate(sketches, axis=0)

    def columns(first, width):
        piece = all_sketch[:, :, first : first + width]
        return piece.transpose(1, 0, 2).reshape(piece.shape[1], heads_kv * width)

    wide = group * hd
    return (
        query_grad, key_grad, value_grad,
        columns(0, wide), columns(wide, hd), columns(wide + hd, hd), columns(wide + 2 * hd, wide),
    )


def solution(mesh):
    split = P("seq", "head")
    by_head = P("head", None)
    in_specs = (split, by_head, split, by_head, split, split, split, split, P(), P())
    return jax.shard_map(
        per_device, mesh=mesh, in_specs=in_specs, out_specs=(split,) * 7, check_vma=False
    )
```

```python
import functools
import math

import jax
import jax.numpy as jnp
from jax import lax
from jax.experimental import pallas as pl
from jax.experimental.pallas import tpu as pltpu
from jax.sharding import PartitionSpec as P

WINDOW = 1024
SCALE = 168.0 ** (-0.5)
EPSILON = 1e-06
ROPE_BASE = 10000.0
NT = (((1,), (1,)), ((), ()))
MESH = pl.DeviceIdType.MESH


def remote(src, dst, send_sem, recv_sem, target):
    return pltpu.make_async_remote_copy(
        src_ref=src, dst_ref=dst, send_sem=send_sem, recv_sem=recv_sem,
        device_id={"seq": target}, device_id_type=MESH,
    )


def dot(a, b):
    return jnp.dot(a, b, preferred_element_type=jnp.float32)


def dot_nt(a, b):
    return lax.dot_general(a, b, NT, preferred_element_type=jnp.float32)


def swap_halves(x):
    return pltpu.roll(x, x.shape[-1] // 2, 1)


def norm_parts(raw):
    rstd = lax.rsqrt(jnp.mean(raw * raw, axis=-1, keepdims=True) + EPSILON)
    return raw * rstd, rstd


def rotate(normed, cos, sin):
    return normed * cos + swap_halves(normed) * sin


def prepare_back(grad, unit, rstd, gain, cos, sin):
    inner = (grad * cos + swap_halves(grad * sin)) * gain
    return rstd * (inner - unit * jnp.mean(inner * unit, axis=-1, keepdims=True))


def attention_kernel(
    count, packed, cos, sin, q_gain, k_gain, x_own, dy_t, q, d_out, k_all, v_all, k_own, v_own,
    query_out, key_out, value_out, *rest
):
    sketch_outs = rest[: 4 if packed else 1]
    rest = rest[len(sketch_outs) :]
    (k_s, v_s, kt_s, vt_s, dk_s, dv_s, e_s, dp_s, p_s, ds_s, sk_s, halo_land, ret_send, ret_land,
     own_s, x_land, halo_ss, halo_rs, ret_ss, ret_rs, x_ss, x_rs) = rest[:22]
    if packed:
        sk_send, sk_land, sk_ss, sk_rs = rest[22:]
    tok = q.shape[0]
    hd = q_gain.shape[1]
    group = q.shape[1] // hd
    sub = tok // 2
    span = 3 * tok
    band = 5 * sub
    cols = group * sub
    exponent = SCALE * math.log2(math.e)
    g = pl.program_id(0)
    heads = k_all.shape[1] // hd
    me = lax.axis_index("seq")

    def halo_copy(dist, kind, head):
        src = (k_all, v_all)[kind].at[:, pl.ds(pl.multiple_of(head * hd, hd), hd)]
        return remote(src, halo_land.at[dist - 1, kind, head], halo_ss.at[dist - 1, kind, head],
                      halo_rs.at[dist - 1, kind, head], lax.rem(me + dist, count))

    def x_copy(dist):
        return remote(x_own, x_land.at[dist - 1], x_ss.at[dist - 1], x_rs.at[dist - 1],
                      lax.rem(me + dist, count))

    def ret_copy(dist, head):
        return remote(ret_send.at[dist - 1, head], ret_land.at[dist - 1, head],
                      ret_ss.at[dist - 1, head], ret_rs.at[dist - 1, head],
                      lax.rem(me - dist + count, count))

    def sketch_copy(step, head):
        to = lax.rem(me + step, count)
        return remote(sk_send.at[head, to], sk_land.at[head, me], sk_ss.at[head, step],
                      sk_rs.at[head, step], to)

    @pl.when(g == 0)
    def _():
        barrier = pltpu.get_barrier_semaphore()

        @pl.loop(1, count)
        def _(step):
            pl.semaphore_signal(barrier, inc=1, device_id={"seq": lax.rem(me + step, count)},
                                device_id_type=MESH)

        pl.semaphore_wait(barrier, count - 1)
        for dist in (1, 2):
            @pl.when(me + dist < count)
            def _():
                x_copy(dist).start()

        @pl.loop(0, heads)
        def _(head):
            for dist in (1, 2):
                @pl.when(me + dist < count)
                def _():
                    halo_copy(dist, 0, head).start()
                    halo_copy(dist, 1, head).start()

        for dist in (1, 2):
            @pl.when(me < dist)
            def _():
                halo_land[dist - 1] = jnp.zeros(halo_land.shape[1:], jnp.bfloat16)
                x_land[dist - 1] = jnp.zeros(x_land.shape[1:], jnp.bfloat16)

            @pl.when(me + dist >= count)
            def _():
                ret_land[dist - 1] = jnp.zeros(ret_land.shape[1:], jnp.bfloat16)

    for dist in (1, 2):
        @pl.when(me >= dist)
        def _():
            halo_copy(dist, 0, g).wait_recv()
            halo_copy(dist, 1, g).wait_recv()

    valid = (jnp.where(me >= 1, 1.0, 0.0), jnp.where(me >= 2, 1.0, 0.0))
    near = (halo_land.at[0, 0, g], halo_land.at[0, 1, g])
    far = (halo_land.at[1, 0, g], halo_land.at[1, 1, g])

    for part, raw, val in ((0, far[0], far[1]), (1, near[0], near[1]), (2, k_own, v_own)):
        rows = pl.ds(part * tok, tok)
        unit, _ = norm_parts(raw[...].astype(jnp.float32))
        prep = rotate(unit * k_gain[...], cos[rows, :], sin[rows, :])
        k_s[rows, :] = prep.astype(jnp.bfloat16)
        kt_s[:, part * tok : (part + 1) * tok] = prep.T.astype(jnp.bfloat16)
        v_s[rows, :] = val[...]
        vt_s[:, part * tok : (part + 1) * tok] = val[...].astype(jnp.float32).T.astype(jnp.bfloat16)

    key_at = lax.broadcasted_iota(jnp.int32, (sub, cols), 0)
    query_at = lax.broadcasted_iota(jnp.int32, (sub, cols), 1) % sub
    older = key_at > query_at
    weight = jnp.where(older, valid[1], 1.0)

    for i in range(2):
        rows = slice(i * sub, (i + 1) * sub)
        own_rows = pl.ds(2 * tok + i * sub, sub)
        q_cos, q_sin = cos[own_rows, :], sin[own_rows, :]
        units = []
        preps = []
        for h in range(group):
            unit, rstd = norm_parts(q[rows, h * hd : (h + 1) * hd].astype(jnp.float32))
            units.append((unit, rstd))
            preps.append(rotate(unit * q_gain[...], q_cos, q_sin).astype(jnp.bfloat16))
        query = jnp.concatenate(preps, axis=0)
        grad = jnp.concatenate([d_out[rows, h * hd : (h + 1) * hd] for h in range(group)], axis=0)

        total = jnp.zeros((1, cols), jnp.float32)
        mixed = jnp.zeros((1, cols), jnp.float32)
        for t in range(4):
            at = slice((i + t) * sub, (i + t + 1) * sub)
            score = dot_nt(k_s[at, :], query)
            grad_p = dot_nt(v_s[at, :], grad)
            if t == 0:
                last = slice((i + 4) * sub, (i + 5) * sub)
                score = jnp.where(older, score, dot_nt(k_s[last, :], query))
                grad_p = jnp.where(older, grad_p, dot_nt(v_s[last, :], grad))
            e = jnp.exp2(score * exponent)
            here = slice(t * sub, (t + 1) * sub)
            e_s[i, here, :] = e
            dp_s[i, here, :] = grad_p
            mixed = mixed + jnp.sum(e * grad_p, axis=0, keepdims=True)
            if t == 0:
                total = total + jnp.sum(e * weight, axis=0, keepdims=True)
            else:
                part = jnp.sum(e, axis=0, keepdims=True)
                shard = (i + t) // 2
                total = total + (part if shard == 2 else part * valid[1 - shard])
        inverse = 1.0 / total
        delta = mixed * inverse
        for t in range(4):
            here = slice(t * sub, (t + 1) * sub)
            prob = e_s[i, here, :] * inverse
            ds = prob * (dp_s[i, here, :] - delta)
            if t == 0:
                last = slice(4 * sub, 5 * sub)
                p_s[i, here, :] = jnp.where(older, prob, 0.0).astype(jnp.bfloat16)
                p_s[i, last, :] = jnp.where(older, 0.0, prob).astype(jnp.bfloat16)
                ds_s[i, here, :] = jnp.where(older, ds, 0.0).astype(jnp.bfloat16)
                ds_s[i, last, :] = jnp.where(older, 0.0, ds).astype(jnp.bfloat16)
            else:
                p_s[i, here, :] = prob.astype(jnp.bfloat16)
                ds_s[i, here, :] = ds.astype(jnp.bfloat16)

        keys = slice(i * sub, i * sub + band)
        dv = dot(p_s[i], grad)
        dk = dot(ds_s[i], query)
        if i == 0:
            dv_s[:band, :] = dv
            dk_s[:band, :] = dk
            dv_s[band:, :] = jnp.zeros((span - band, hd), jnp.float32)
            dk_s[band:, :] = jnp.zeros((span - band, hd), jnp.float32)
        else:
            dv_s[keys, :] += dv
            dk_s[keys, :] += dk
        attn_t = dot(vt_s[:, keys], p_s[i]).astype(jnp.bfloat16)
        dq = dot(kt_s[:, keys], ds_s[i]).T * SCALE
        for h in range(group):
            unit, rstd = units[h]
            part = prepare_back(
                dq[h * sub : (h + 1) * sub, :], unit, rstd, q_gain[...], q_cos, q_sin
            ).astype(jnp.bfloat16)
            query_out[rows, h * hd : (h + 1) * hd] = part
            sk_q = dot(x_own[:, rows], part)
            sk_o = dot_nt(dy_t[:, rows], attn_t[:, h * sub : (h + 1) * sub])
            to_q = slice(h * hd, (h + 1) * hd)
            to_o = slice((group + 2 + h) * hd, (group + 3 + h) * hd)
            if i == 0:
                sk_s[:, to_q] = sk_q
                sk_s[:, to_o] = sk_o
            else:
                sk_s[:, to_q] += sk_q
                sk_s[:, to_o] += sk_o

    @pl.when(g == 0)
    def _():
        for dist in (1, 2):
            @pl.when(me >= dist)
            def _():
                x_copy(dist).wait_recv()

    sk_k = jnp.zeros((x_own.shape[0], hd), jnp.float32)
    sk_v = jnp.zeros((x_own.shape[0], hd), jnp.float32)
    for part, raw, out in ((0, far[0], ret_send.at[1, g]), (1, near[0], ret_send.at[0, g]),
                           (2, k_own, own_s.at[g])):
        rows = pl.ds(part * tok, tok)
        unit, rstd = norm_parts(raw[...].astype(jnp.float32))
        dk = prepare_back(
            dk_s[rows, :] * SCALE, unit, rstd, k_gain[...], cos[rows, :], sin[rows, :]
        )
        dv = dv_s[rows, :]
        out[0] = dk.astype(out.dtype)
        out[1] = dv.astype(out.dtype)
        xs = x_own[...] if part == 2 else x_land[1 - part]
        sk_k = sk_k + dot(xs, dk.astype(jnp.bfloat16))
        sk_v = sk_v + dot(xs, dv.astype(jnp.bfloat16))
    for dist in (2, 1):
        @pl.when(me >= dist)
        def _():
            ret_copy(dist, g).start()
    sk_s[:, group * hd : (group + 1) * hd] = sk_k
    sk_s[:, (group + 1) * hd : (group + 2) * hd] = sk_v

    width = sk_s.shape[1]
    if packed:
        mid = width // 2
        parts = sk_s[...].reshape(count, 8, width)
        sk_send[g] = jnp.concatenate([parts[:, :, :mid], parts[:, :, mid:]], axis=1).astype(
            jnp.bfloat16)
        sk_land[g, me] = sk_send[g, me]

        @pl.loop(1, count)
        def _(step):
            sketch_copy(step, g).start()
    else:
        sketch_outs[0][0] = sk_s[...]

    @pl.when(g == heads - 1)
    def _():
        @pl.loop(0, heads)
        def _(head):
            for dist in (1, 2):
                @pl.when(me + dist < count)
                def _():
                    halo_copy(dist, 0, head).wait_send()
                    halo_copy(dist, 1, head).wait_send()
                    ret_copy(dist, head).wait_recv()

                @pl.when(me >= dist)
                def _():
                    ret_copy(dist, head).wait_send()

        for dist in (1, 2):
            @pl.when(me + dist < count)
            def _():
                x_copy(dist).wait_send()

        for h in range(heads):
            at = slice(h * hd, (h + 1) * hd)
            for kind, out in ((0, key_out), (1, value_out)):
                out[:, at] = (own_s[h, kind] + ret_land[0, h, kind].astype(jnp.float32)
                              + ret_land[1, h, kind].astype(jnp.float32)).astype(jnp.bfloat16)

        if packed:
            @pl.loop(0, heads)
            def _(head):
                @pl.loop(1, count)
                def _(step):
                    sketch_copy(step, head).wait()

            mid = width // 2
            wide = group * hd
            for h in range(heads):
                both = jnp.sum(sk_land[h].astype(jnp.float32), axis=0)
                row = jnp.concatenate([both[:8], both[8:]], axis=1)
                sketch_outs[0][:, h * wide : (h + 1) * wide] = row[:, :wide]
                sketch_outs[1][:, h * hd : (h + 1) * hd] = row[:, wide : wide + hd]
                sketch_outs[2][:, h * hd : (h + 1) * hd] = row[:, wide + hd : wide + 2 * hd]
                sketch_outs[3][:, h * wide : (h + 1) * wide] = row[:, wide + 2 * hd :]


def attention(count, cos, sin, q_gain, k_gain, x_t, dy_t, q_raw, d_out, k_raw, values):
    tok, q_cols = q_raw.shape
    kv_cols = k_raw.shape[1]
    hd = q_gain.shape[1]
    heads = kv_cols // hd
    group = q_cols // kv_cols
    rank = x_t.shape[0]
    packed = rank == 8 * count
    wide = group * hd
    width = 2 * wide + 2 * hd
    span, sub = 3 * tok, tok // 2
    cols = group * sub
    bf16, f32 = jnp.bfloat16, jnp.float32
    whole = lambda *shape: pl.BlockSpec(shape, lambda g: (0,) * len(shape))
    q_spec = pl.BlockSpec((tok, wide), lambda g: (0, g))
    k_spec = pl.BlockSpec((tok, hd), lambda g: (0, g))
    hbm = pl.BlockSpec(memory_space=pl.ANY)
    out_specs = [q_spec, whole(tok, kv_cols), whole(tok, kv_cols)]
    out_shape = [
        jax.ShapeDtypeStruct(q_raw.shape, bf16),
        jax.ShapeDtypeStruct(k_raw.shape, bf16),
        jax.ShapeDtypeStruct(k_raw.shape, bf16),
    ]
    scratch = [
        pltpu.VMEM((span, hd), bf16),
        pltpu.VMEM((span, hd), bf16),
        pltpu.VMEM((hd, span), bf16),
        pltpu.VMEM((hd, span), bf16),
        pltpu.VMEM((span, hd), f32),
        pltpu.VMEM((span, hd), f32),
        pltpu.VMEM((2, 4 * sub, cols), f32),
        pltpu.VMEM((2, 4 * sub, cols), f32),
        pltpu.VMEM((2, 5 * sub, cols), bf16),
        pltpu.VMEM((2, 5 * sub, cols), bf16),
        pltpu.VMEM((rank, width), f32),
        pltpu.VMEM((2, 2, heads, tok, hd), bf16),
        pltpu.VMEM((2, heads, 2, tok, hd), bf16),
        pltpu.VMEM((2, heads, 2, tok, hd), bf16),
        pltpu.VMEM((heads, 2, tok, hd), f32),
        pltpu.VMEM((2, rank, tok), bf16),
        pltpu.SemaphoreType.DMA((2, 2, heads)),
        pltpu.SemaphoreType.DMA((2, 2, heads)),
        pltpu.SemaphoreType.DMA((2, heads)),
        pltpu.SemaphoreType.DMA((2, heads)),
        pltpu.SemaphoreType.DMA((2,)),
        pltpu.SemaphoreType.DMA((2,)),
    ]
    if packed:
        for n in (wide, hd, hd, wide):
            out_specs.append(whole(8, heads * n))
            out_shape.append(jax.ShapeDtypeStruct((8, heads * n), f32))
        scratch += [
            pltpu.VMEM((heads, count, 16, width // 2), bf16),
            pltpu.VMEM((heads, count, 16, width // 2), bf16),
            pltpu.SemaphoreType.DMA((heads, count)),
            pltpu.SemaphoreType.DMA((heads, count)),
        ]
    else:
        out_specs.append(pl.BlockSpec((1, rank, width), lambda g: (g, 0, 0)))
        out_shape.append(jax.ShapeDtypeStruct((heads, rank, width), f32))
    return pl.pallas_call(
        functools.partial(attention_kernel, count, packed),
        grid=(heads,),
        in_specs=[whole(span, hd), whole(span, hd), whole(1, hd), whole(1, hd),
                  whole(rank, tok), whole(rank, tok), q_spec, q_spec, hbm, hbm, k_spec, k_spec],
        out_specs=out_specs,
        out_shape=out_shape,
        scratch_shapes=scratch,
        compiler_params=pltpu.CompilerParams(
            dimension_semantics=("arbitrary",), vmem_limit_bytes=56 * 1024 * 1024,
            collective_id=0, has_side_effects=True,
        ),
        cost_estimate=pl.CostEstimate(
            flops=heads * 20 * 5 * sub * tok * group * hd,
            bytes_accessed=heads * 4 * tok * hd * 20,
            transcendentals=heads * 4 * sub * tok * group,
        ),
    )(cos, sin, q_gain, k_gain, x_t, dy_t, q_raw, d_out, k_raw, values, k_raw, values)


def scatter_sum(part, order):
    count = lax.axis_size("seq")
    bits = len(order)
    heads, rank, cols = part.shape
    me = lax.axis_index("seq")
    cur = part.reshape((heads,) + (2,) * bits + (rank // count, cols))
    axes = list(range(bits - 1, -1, -1))
    for bit in order:
        axis = 1 + axes.index(bit)
        axes.remove(bit)
        mine = (me >> bit) & 1
        keep = lax.dynamic_index_in_dim(cur, mine, axis, keepdims=False)
        away = lax.dynamic_index_in_dim(cur, 1 - mine, axis, keepdims=False)
        pairs = [(i, i ^ (1 << bit)) for i in range(count)]
        cur = keep + lax.ppermute(away.astype(jnp.bfloat16), "seq", pairs).astype(jnp.float32)
    return cur


def per_device(
    layer_input, omega_in, upstream, omega_out, q_raw, k_raw, values, d_out, q_gain, k_gain
):
    tok = q_raw.shape[0]
    hd = q_gain.shape[0]
    kv_cols = k_raw.shape[1]
    heads_kv = kv_cols // hd
    group = q_raw.shape[1] // kv_cols
    me = lax.axis_index("seq")
    count = lax.axis_size("seq")

    partial_x = dot(layer_input, omega_in)
    partial_y = dot(upstream, omega_out)
    summed_x, summed_y = lax.psum((partial_x, partial_y), "head")
    x_t = summed_x.astype(jnp.bfloat16).T
    dy_t = summed_y.astype(jnp.bfloat16).T

    half = hd // 2
    inverse_freq = ROPE_BASE ** (-(jnp.arange(half, dtype=jnp.float32) * 2.0 / hd))
    positions = (me - 2) * tok + jnp.arange(3 * tok, dtype=jnp.int32)
    angles = positions.astype(jnp.float32)[:, None] * inverse_freq[None, :]
    cos, sin = jnp.cos(angles), jnp.sin(angles)
    cos = jnp.concatenate([cos, cos], axis=1)
    sin = jnp.concatenate([-sin, sin], axis=1)
    results = attention(
        count, cos, sin, q_gain[None, :], k_gain[None, :], x_t, dy_t, q_raw, d_out, k_raw, values
    )
    if len(results) == 7:
        return tuple(results)
    query_grad, key_grad, value_grad, sketch = results
    all_sketch = scatter_sum(sketch, list(range(count.bit_length() - 1)))

    def columns(first, width):
        piece = all_sketch[:, :, first : first + width]
        return piece.transpose(1, 0, 2).reshape(piece.shape[1], heads_kv * width)

    wide = group * hd
    return (
        query_grad, key_grad, value_grad,
        columns(0, wide), columns(wide, hd), columns(wide + hd, hd), columns(wide + 2 * hd, wide),
    )


def solution(mesh):
    split = P("seq", "head")
    by_head = P("head", None)
    in_specs = (split, by_head, split, by_head, split, split, split, split, P(), P())
    return jax.shard_map(
        per_device, mesh=mesh, in_specs=in_specs, out_specs=(split,) * 7, check_vma=False
    )
```
